32 devices in a mesh: groups: 2 (over y), expert: 4 (over z), dp: 4 (over x, core).
Axes of the slice: x: 2, y: 2, z: 4, core: 2. Of those that a mesh axis runs over, the one named last changes fastest.
Arguments:
- tokens: bfloat16 [1024, 2048], P(('groups', 'expert', 'dp')), parts along dimension 0, may hold values from -6 to 6
- routing: int32 [1024, 2], P(('groups', 'expert', 'dp')), parts along dimension 0, may hold values from 0 to 3, all different within a row; in each aligned block of 32 rows (0 to 31, 32 to 63, ...) at most 32 rows name the same one
- gates: float32 [1024, 2], P(('groups', 'expert', 'dp')), parts along dimension 0, may hold values from 0.5 to 1.5
- ln_gain: float32 [2048], replicated, may hold values from 0.1 to 1.9
- w_in: bfloat16 [4, 2048, 4096], P('expert', None, 'dp'), may hold values from -0.125 to 0.125
- w_out: bfloat16 [4, 4096, 2048], P('expert', 'dp'), may hold values from -0.09375 to 0.09375
Outputs:
- mixed: bfloat16 [1024, 2048], P(('groups', 'expert', 'dp')), parts along dimension 0
The draws below stay inside these ranges and needn't reach their ends.
There are 2 independent parts, one for each index of `groups`. The reference program is written for one: setup_inputs(seed, part) draws one part's arguments, and reference() takes and returns one part's arrays. A program takes and returns all parts, laid end to end along the dimension named above; an argument that names none is the same for every part. Nothing has to cross between parts.
Inputs may be any that keep to these rules, and one draw needn't show every extreme that they name: `routing`: the 32 rows of one device name each expert at most 32 times, a bound that some block reaches; a row's two experts differ.
All inputs are finite; a program needn't handle non-finite values.
Results may differ from the reference program's by a relative error of at most 0.006.
Values may be sent and summed in bfloat16 or wider, within the bound.
No kernel may reach another device: no remote copies, remote signals or barrier semaphores. Data moves between devices by JAX's collectives and lax.ppermute only.
A program may use at most 64 MiB of HBM per device.

```python
import math
import jax
import jax.numpy as jnp
import numpy as np
from jax import lax

D = 2048
TOPK = 2
FF_WIN = 4096
TOK_DEV = 32
EXPERTS = 4
FF_DEV = 1024
CAP = 32
TOKENS = 512
N_EXPERT = 4
N_DP = 4


def levels(own_key, shape, split, smallest, top_value):
    loudness = 1.0
    for axis_at, shards_of in split:
        draws = jax.random.uniform(jax.random.fold_in(jax.random.fold_in(own_key, 6), axis_at), (shards_of,), jnp.float32, smallest / len(split), top_value / len(split))
        loudness = loudness * jnp.repeat(jnp.exp(draws), shape[axis_at] // shards_of).reshape((-1,) + (1,) * (len(shape) - 1 - axis_at))
    return loudness


def shared_out(rng, own, number, rows, number_of, top, most, slope):
    sequence = jax.random.permutation(rng, number_of)
    crowded, ordinary = portions_of(number_of, rows * top, most, slope, True), portions_of(number_of, rows * top, most, slope, False)
    places = jnp.arange(number_of)

    def named(tallies, rotation):
        used = int((tallies > 0).sum())
        fixed = max(1, used // 4)
        shifted = fixed + (places - fixed + rotation * (used - fixed)) % max(1, number_of - fixed)
        return jnp.zeros((number_of,), jnp.int32).at[sequence[jnp.where(places < fixed, places, shifted)]].set(jnp.asarray(tallies, jnp.int32))

    tallies = jnp.where(number % 4 == 0, named(crowded, number // 4), named(ordinary, number - number // 4 - 1))
    mixed = jax.random.permutation(jax.random.fold_in(own, 3), number_of)
    donor, sink = mixed[0:number_of // 2 * 2:2], mixed[1:number_of // 2 * 2:2]
    room = jnp.minimum(tallies[donor] - 1, most - tallies[sink]) // 2
    room = jnp.where((donor == sequence[0]) | (sink == sequence[0]) | (tallies[sink] == 0), 0, jnp.maximum(room, 0))
    shifted = jax.random.randint(jax.random.fold_in(own, 4), (number_of // 2,), 0, 1 << 20) % (room + 1)
    tallies = tallies.at[donor].add(-shifted).at[sink].add(shifted)
    members = jnp.searchsorted(jnp.cumsum(tallies), jnp.arange(rows * top), side="right").astype(jnp.int32)
    table = members.reshape(top, rows).T
    table = table[jax.random.permutation(jax.random.fold_in(own, 1), rows)]
    rotation = jax.random.randint(jax.random.fold_in(own, 2), (rows, 1), 0, top)
    return jnp.take_along_axis(table, (jnp.arange(top)[None, :] + rotation) % top, axis=1)


def portions_of(amount, total, bound, lean, full):
    portions = [(1 << 20) // math.isqrt(standing ** lean) + 1 for standing in range(1, amount + 1)]
    largest = bound if full else min(bound, max(-(-total // amount), total * portions[0] // sum(portions)))
    least = 1 if total - largest >= amount - 1 else 0
    counts, spare = [largest] + [least] * (amount - 1), total - largest - least * (amount - 1)
    while spare > 0:
        free = [i for i in range(1, amount) if counts[i] < largest] or [i for i in range(1, amount) if counts[i] < bound]
        whole, remaining = sum([portions[i] for i in free]), spare
        for i in free:
            more = min(bound - counts[i], max(1, remaining * portions[i] // whole), spare)
            counts[i] = counts[i] + more
            spare = spare - more
    return np.array(counts)


def scatter_about(rng, dims, scale, bound, shards=(), held_as=jnp.bfloat16):
    values = scale * jax.random.normal(rng, dims, jnp.float32)
    if shards:
        values = values * levels(rng, dims, shards, -0.22, 0.18)
    return jnp.clip(values, -bound, bound).astype(held_as)


def setup_inputs(seed: int = 0, part: int = 0) -> dict:
    keys = jax.random.split(jax.random.key(seed), 7)
    part_splits = jax.random.split(jax.random.fold_in(keys[6], part), 7)
    tokens = scatter_about(part_splits[0], (TOKENS, D), 1.0, 6.0, ((0, 16),))
    routing_keys = jax.random.split(jax.random.fold_in(part_splits[1], 1), TOKENS // TOK_DEV)
    routing_turns = jax.random.permutation(jax.random.fold_in(part_splits[1], 3), TOKENS // TOK_DEV)
    routing = jax.vmap(lambda own, number: shared_out(jax.random.fold_in(part_splits[1], 2), own, number, TOK_DEV, EXPERTS, TOPK, CAP, 2))(routing_keys, routing_turns).reshape((TOKENS, TOPK))
    gates = jnp.clip(0.5 + 1.0 * jax.random.uniform(part_splits[2], (TOKENS, TOPK), jnp.float32) ** levels(part_splits[2], (TOKENS, TOPK), ((0, 16),), -0.2, 0.2), 0.5, 1.5)
    ln_gain = jnp.clip(1.0 + 0.18 * jax.random.normal(keys[3], (D,), jnp.float32), 0.1, 1.9)
    w_in = scatter_about(keys[4], (EXPERTS, D, FF_WIN), D ** -0.5, 0.125, ((0, 4), (2, 4)))
    w_out = scatter_about(keys[5], (EXPERTS, FF_WIN, D), FF_WIN ** -0.5, 0.09375, ((0, 4), (1, 4)))
    return {"tokens": tokens, "routing": routing, "gates": gates, "ln_gain": ln_gain, "w_in": w_in, "w_out": w_out}


def layer_norm(tokens, ln_gain):
    values = tokens.astype(jnp.float32)
    center = values - lax.optimization_barrier(jnp.mean(values, axis=1, keepdims=True))
    variance = lax.optimization_barrier(jnp.mean(center * center, axis=1, keepdims=True))
    return (center * lax.rsqrt(variance + 1e-05) * ln_gain).astype(jnp.bfloat16)

def reference(tokens, routing, gates, ln_gain, w_in, w_out):
    normed = layer_norm(tokens, ln_gain)
    flat_ids = routing.reshape(-1)
    flat_gates = gates.reshape(-1)
    limit = N_EXPERT * N_DP * CAP

    def one_expert(accum, expert):
        found = jnp.nonzero(flat_ids == expert, size=limit, fill_value=-1)[0].astype(jnp.int32)
        valid_row = found >= 0
        safe_idx = jnp.where(valid_row, found, 0).astype(jnp.int32)
        row_mat = normed[safe_idx // 2]

        def one_block(block, total):
            start = (block * FF_DEV).astype(jnp.int32)
            w_first = lax.dynamic_slice_in_dim(w_in[expert], start, FF_DEV, 1)
            w_second = lax.dynamic_slice_in_dim(w_out[expert], start, FF_DEV, 0)
            hidden = jnp.maximum(jnp.dot(row_mat, w_first, preferred_element_type=jnp.float32), 0.0).astype(jnp.bfloat16)
            product = jnp.dot(hidden, w_second, preferred_element_type=jnp.float32).astype(jnp.bfloat16)
            return total + product.astype(jnp.float32)
        summed_rows = lax.fori_loop(jnp.int32(0), jnp.int32(N_DP), one_block, jnp.zeros((limit, tokens.shape[1]), jnp.float32))
        expert_rows = lax.optimization_barrier(summed_rows.astype(jnp.bfloat16))
        weight = jnp.where(valid_row, flat_gates[safe_idx], jnp.zeros_like(flat_gates[safe_idx]))
        accum = accum.at[safe_idx // 2].add(expert_rows.astype(jnp.float32) * weight[:, None])
        return (accum, None)
    start_sum = jnp.zeros(tokens.shape, jnp.float32)
    accum, unused = lax.scan(one_expert, start_sum, jnp.arange(EXPERTS, dtype=jnp.int32))
    return (tokens.astype(jnp.float32) + accum).astype(jnp.bfloat16)
```

```python
import functools

import jax
import jax.numpy as jnp
from jax import lax
from jax.experimental import pallas as pl
from jax.experimental.pallas import tpu as pltpu
from jax.sharding import PartitionSpec as P

LANES = 128
GATE_TERMS = 3


def norm_kernel(experts, tokens_ref, routing_ref, gates_ref, gain_ref, out_ref):
    width = tokens_ref.shape[1]
    values = tokens_ref[...].astype(jnp.float32)
    center = values - jnp.mean(values, axis=1, keepdims=True)
    variance = jnp.mean(center * center, axis=1, keepdims=True)
    normed = center * lax.rsqrt(variance + 1e-05) * gain_ref[...]
    out_ref[:, :width] = normed.astype(jnp.bfloat16)
    lane = lax.broadcasted_iota(jnp.int32, (tokens_ref.shape[0], LANES), 1)
    expert = lax.rem(lane, experts)
    term = lax.div(lane, experts)
    gate = jnp.zeros(lane.shape, jnp.float32)
    for k in range(routing_ref.shape[1]):
        gate += jnp.where(routing_ref[:, k : k + 1] == expert, gates_ref[:, k : k + 1], 0.0)
    rest = gate
    packed = jnp.zeros(lane.shape, jnp.float32)
    for i in range(GATE_TERMS):
        part = rest.astype(jnp.bfloat16).astype(jnp.float32)
        packed = jnp.where(term == i, part, packed)
        rest = rest - part
    out_ref[:, width:] = packed.astype(jnp.bfloat16)


def norm_and_pack(tokens, routing, gates, ln_gain, experts):
    rows, width = tokens.shape
    return pl.pallas_call(
        functools.partial(norm_kernel, experts),
        out_shape=jax.ShapeDtypeStruct((rows, width + LANES), jnp.bfloat16),
        name="norm",
    )(tokens, routing, gates, ln_gain.reshape(1, width))


def ffn_kernel(experts, pieces, expert_ref, *refs):
    kept, sent = refs[:pieces], refs[pieces : 2 * pieces]
    w_first, w_second = refs[2 * pieces : 2 * pieces + 2]
    keep_ref, send_ref, rows_ref, hidden_ref = refs[2 * pieces + 2 :]
    width, units = w_first.shape
    at = 0
    for ref in kept + sent:
        rows_ref[at : at + ref.shape[0], :] = ref[...]
        at += ref.shape[0]
    half = at // 2
    lane = lax.broadcasted_iota(jnp.int32, (at, LANES), 1)
    chosen = (lax.rem(lane, experts) == expert_ref[0]) & (lane < GATE_TERMS * experts)
    tail = rows_ref[:, width:].astype(jnp.float32)
    gate = jnp.sum(jnp.where(chosen, tail, 0.0), axis=1, keepdims=True)
    step = 256
    for j in range(0, units, step):
        dot = jnp.dot(
            rows_ref[:, :width], w_first[:, j : j + step], preferred_element_type=jnp.float32
        )
        hidden_ref[:, j : j + step] = jnp.maximum(dot, 0.0).astype(jnp.bfloat16)
    for j in range(0, width, step):
        dot = jnp.dot(
            hidden_ref[...], w_second[:, j : j + step], preferred_element_type=jnp.float32
        )
        out = (dot * gate).astype(jnp.bfloat16)
        send_ref[:, j : j + step] = out[half:]
        keep_ref[:, j : j + step] = out[:half]


def ffn(kept, sent, w_first, w_second, experts, expert):
    width, units = w_first.shape
    half = sum(a.shape[0] for a in kept)
    out = jax.ShapeDtypeStruct((half, width), jnp.bfloat16)
    vmem = pl.BlockSpec(memory_space=pltpu.VMEM)
    count = len(kept)
    return pl.pallas_call(
        functools.partial(ffn_kernel, experts, count),
        out_shape=(out, out),
        in_specs=[pl.BlockSpec(memory_space=pltpu.SMEM)] + [vmem] * (2 * count + 2),
        out_specs=(vmem, vmem),
        scratch_shapes=[
            pltpu.VMEM((2 * half, width + LANES), jnp.bfloat16),
            pltpu.VMEM((2 * half, units), jnp.bfloat16),
        ],
        compiler_params=pltpu.CompilerParams(vmem_limit_bytes=32 * 1024 * 1024),
        cost_estimate=pl.CostEstimate(
            flops=8 * half * width * units, bytes_accessed=4 * width * units, transcendentals=0
        ),
        name="ffn",
    )(expert, *kept, *sent, w_first, w_second)


def swap(array, axis, distance):
    pairs = [(i, i ^ distance) for i in range(lax.axis_size(axis))]
    return lax.ppermute(array, axis, pairs)


def add(*arrays):
    return sum(a.astype(jnp.float32) for a in arrays)


GROUPS = ((0, 1), (2, 3))


def dense_body(tokens, routing, gates, ln_gain, w_in, w_out):
    rows = tokens.shape[0]
    experts = lax.axis_size("expert")
    core_bit, chip_bit = 1, 2
    w_first, w_second = w_in[0], w_out[0]
    expert = lax.axis_index("expert").reshape(1)
    own = norm_and_pack(tokens, routing, gates, ln_gain, experts)
    lane = [own] + [swap(own, "expert", k) for k in range(1, experts)]
    across = [swap(a, "dp", chip_bit) for a in lane]
    lane_other = [swap(a, "dp", core_bit) for a in lane]
    across_other = [swap(a, "dp", core_bit) for a in across]
    total = [None] * experts
    for group in GROUPS:
        kept = [lane[k] for k in group] + [across[k] for k in group]
        sent = [lane_other[k] for k in group] + [across_other[k] for k in group]
        keep, send = ffn(kept, sent, w_first, w_second, experts, expert)
        back = swap(send, "dp", core_bit)
        half = keep.shape[0] // 2
        far = add(keep[half:], back[half:]).astype(jnp.bfloat16)
        far_back = swap(far, "dp", chip_bit)
        for i, k in enumerate(group):
            at = slice(i * rows, (i + 1) * rows)
            if k == 0:
                total[k] = add(keep[at], back[at], far_back[at])
            else:
                block = add(keep[at], back[at], far_back[at]).astype(jnp.bfloat16)
                total[k] = swap(block, "expert", k)
    return add(tokens, *total).astype(jnp.bfloat16)


def layer_norm(tokens, ln_gain):
    values = tokens.astype(jnp.float32)
    center = values - jnp.mean(values, axis=1, keepdims=True)
    variance = jnp.mean(center * center, axis=1, keepdims=True)
    return (center * lax.rsqrt(variance + 1e-05) * ln_gain).astype(jnp.bfloat16)


def slot_index(routing, experts, capacity):
    flat_ids = routing.reshape(-1)
    onehot = (flat_ids[:, None] == jnp.arange(experts, dtype=jnp.int32)[None, :]).astype(jnp.int32)
    rank_run = jnp.cumsum(onehot, axis=0) - 1
    own_rank = jnp.sum(onehot * rank_run, axis=1)
    return flat_ids * capacity + own_rank


def pack_slots(normed, routing, experts, capacity):
    slots = slot_index(routing, experts, capacity)
    picker = (slots[None, :] == jnp.arange(experts * capacity, dtype=jnp.int32)[:, None]).astype(
        jnp.bfloat16
    )
    picker = picker.reshape(experts * capacity, normed.shape[0], routing.shape[1]).sum(axis=2)
    outgoing = jnp.dot(picker, normed, preferred_element_type=jnp.float32).astype(jnp.bfloat16)
    return outgoing.reshape(experts, capacity, normed.shape[1])


def run_experts(block_in, w_first, w_second):
    dims_in = block_in.shape
    row_mat = block_in.reshape(-1, dims_in[-1])
    hidden = jnp.maximum(jnp.dot(row_mat, w_first, preferred_element_type=jnp.float32), 0.0).astype(
        jnp.bfloat16
    )
    product = jnp.dot(hidden, w_second, preferred_element_type=jnp.float32).astype(jnp.bfloat16)
    return product.reshape(dims_in)


def slot_body(tokens, routing, gates, ln_gain, w_in, w_out):
    rows_dev = tokens.shape[0]
    feature_dim = tokens.shape[1]
    top_count = routing.shape[1]
    experts = lax.axis_size("expert")
    dp_size = lax.axis_size("dp")
    capacity = max(2, min(rows_dev, 2 * rows_dev * top_count // experts))
    w_first = w_in[0]
    w_second = w_out[0]
    normed = layer_norm(tokens, ln_gain)
    own_slots = slot_index(routing, experts, capacity)
    all_normed, all_routes = (
        lax.all_gather(normed, "dp", axis=0, tiled=True),
        lax.all_gather(routing, "dp", axis=0, tiled=True),
    )

    def pack_member(member_rows, member_routes):
        return pack_slots(member_rows, member_routes, experts, capacity)

    packed = jax.vmap(pack_member)(
        all_normed.reshape(dp_size, rows_dev, feature_dim),
        all_routes.reshape(dp_size, rows_dev, top_count),
    )
    partials = run_experts(
        lax.all_to_all(packed, "expert", split_axis=1, concat_axis=1, tiled=True), w_first, w_second
    )
    returned = lax.all_to_all(
        lax.all_to_all(partials, "expert", split_axis=1, concat_axis=1, tiled=True),
        "dp",
        split_axis=0,
        concat_axis=0,
        tiled=True,
    )
    block_total = returned.astype(jnp.float32).sum(axis=0)
    expert_out = block_total.astype(jnp.bfloat16).reshape(experts * capacity, feature_dim)
    expert_out = lax.optimization_barrier(expert_out)
    picker = (
        own_slots[:, None] == jnp.arange(experts * capacity, dtype=jnp.int32)[None, :]
    ).astype(jnp.bfloat16)
    values = jnp.dot(picker, expert_out, preferred_element_type=jnp.float32)
    weighted = values.reshape(rows_dev, top_count, feature_dim) * gates[:, :, None]
    return (tokens.astype(jnp.float32) + weighted.sum(axis=1)).astype(jnp.bfloat16)


def body(tokens, routing, gates, ln_gain, w_in, w_out):
    rows_dev = tokens.shape[0]
    experts = lax.axis_size("expert")
    capacity = max(2, min(rows_dev, 2 * rows_dev * routing.shape[1] // experts))
    if capacity == rows_dev and experts == 4 and lax.axis_size("dp") == 4:
        return dense_body(tokens, routing, gates, ln_gain, w_in, w_out)
    return slot_body(tokens, routing, gates, ln_gain, w_in, w_out)


def solution(mesh):
    placed = (
        P(("groups", "expert", "dp"), None),
        P(("groups", "expert", "dp"), None),
        P(("groups", "expert", "dp"), None),
        P(),
        P("expert", None, "dp"),
        P("expert", "dp", None),
    )
    return jax.shard_map(
        body,
        mesh=mesh,
        in_specs=placed,
        out_specs=P(("groups", "expert", "dp"), None),
        check_vma=False,
    )
```

```python
import functools

import jax
import jax.numpy as jnp
from jax import lax
from jax.experimental import pallas as pl
from jax.experimental.pallas import tpu as pltpu
from jax.sharding import PartitionSpec as P

LANES = 128
GATE_TERMS = 3
VMEM = pl.BlockSpec(memory_space=pltpu.VMEM)
SMALL = pltpu.CompilerParams(vmem_limit_bytes=4 * 1024 * 1024)
CHEAP = pl.CostEstimate(flops=1, bytes_accessed=1, transcendentals=0)
DEAR = pl.CostEstimate(flops=10**11, bytes_accessed=1, transcendentals=0)
ANY = pl.BlockSpec(memory_space=pl.ANY)


def in_hbm(array):
    return pltpu.with_memory_space_constraint(array, pltpu.HBM)


def in_vmem(array):
    return pltpu.with_memory_space_constraint(array, pltpu.VMEM)


def norm_kernel(experts, *refs):
    sources, out_ref, targets, sems = refs[:4], refs[4], refs[5:9], refs[9]
    copies = [
        pltpu.make_async_copy(source, target, sems.at[i])
        for i, (source, target) in enumerate(zip(sources, targets))
    ]
    for copy in copies:
        copy.start()
    for copy in copies:
        copy.wait()
    tokens_ref, routing_ref, gates_ref, gain_ref = targets
    width = tokens_ref.shape[1]
    values = tokens_ref[...].astype(jnp.float32)
    center = values - jnp.mean(values, axis=1, keepdims=True)
    variance = jnp.mean(center * center, axis=1, keepdims=True)
    normed = center * lax.rsqrt(variance + 1e-05) * gain_ref[...]
    out_ref[:, :width] = normed.astype(jnp.bfloat16)
    lane = lax.broadcasted_iota(jnp.int32, (LANES, tokens_ref.shape[0]), 0)
    expert = lax.rem(lane, experts)
    term = lax.div(lane, experts)
    gate = jnp.zeros(lane.shape, jnp.float32)
    for k in range(routing_ref.shape[0]):
        gate += jnp.where(routing_ref[k : k + 1, :] == expert, gates_ref[k : k + 1, :], 0.0)
    rest = gate
    packed = jnp.zeros(lane.shape, jnp.float32)
    for i in range(GATE_TERMS):
        part = rest.astype(jnp.bfloat16).astype(jnp.float32)
        packed = jnp.where(term == i, part, packed)
        rest = rest - part
    out_ref[:, width:] = packed.T.astype(jnp.bfloat16)


def norm_and_pack(tokens, routing, gates, ln_gain, experts):
    rows, width = tokens.shape
    arrays = (tokens, routing.T, gates.T, ln_gain.reshape(1, width))
    return pl.pallas_call(
        functools.partial(norm_kernel, experts),
        out_shape=pltpu.VMEM((rows, width + LANES), jnp.bfloat16),
        in_specs=[ANY] * 4,
        out_specs=VMEM,
        scratch_shapes=[pltpu.VMEM(a.shape, a.dtype) for a in arrays]
        + [pltpu.SemaphoreType.DMA((4,))],
        compiler_params=SMALL,
        cost_estimate=CHEAP,
        name="norm",
    )(*[in_hbm(a) for a in arrays])


def join_kernel(pieces, *refs):
    at = 0
    for ref in refs[:pieces]:
        refs[-1][at : at + ref.shape[0], :] = ref[...]
        at += ref.shape[0]


def join(arrays, behind=(), cost=CHEAP):
    rows, width = sum(a.shape[0] for a in arrays), arrays[0].shape[1]
    return pl.pallas_call(
        functools.partial(join_kernel, len(arrays)),
        out_shape=pltpu.VMEM((rows, width), arrays[0].dtype),
        in_specs=[VMEM] * len(arrays) + [ANY] * len(behind),
        out_specs=VMEM,
        compiler_params=SMALL,
        cost_estimate=cost,
        name="join",
    )(*arrays, *behind)


def gate_column(experts, expert_ref, tail):
    lane = lax.broadcasted_iota(jnp.int32, tail.shape, 1)
    chosen = (lax.rem(lane, experts) == expert_ref[0]) & (lane < GATE_TERMS * experts)
    return jnp.sum(jnp.where(chosen, tail.astype(jnp.float32), 0.0), axis=1, keepdims=True)


def load_ffn_kernel(
    experts, cuts, expert_ref, kept_ref, sent_ref, first_ref, second_ref, *refs
):
    keep_ref, send_ref, weights_ref, rows_ref, hidden_ref, total_ref, sems = refs
    width, units = first_ref.shape
    copies = []
    for j in range(cuts):
        size = width // cuts
        part = pl.ds(j * size, size)
        copies.append(
            [pltpu.make_async_copy(first_ref.at[part], weights_ref.at[part], sems.at[0, j])]
        )
    panels = second_ref.shape[1] // units
    for j in range(cuts):
        size = units // cuts
        copies.append(
            [
                pltpu.make_async_copy(
                    second_ref.at[pl.ds(j * size, size), pl.ds(i * units, units)],
                    weights_ref.at[pl.ds(width + i * units + j * size, size)],
                    sems.at[1 + i, j],
                )
                for i in range(panels)
            ]
        )
    for group in copies:
        for copy in group:
            copy.start()
    half = kept_ref.shape[0]
    rows_ref[:half, :] = kept_ref[...]
    rows_ref[half:, :] = sent_ref[...]
    gate = gate_column(experts, expert_ref, rows_ref[:, width:])
    for j in range(cuts):
        for copy in copies[j]:
            copy.wait()
        size = width // cuts
        part = slice(j * size, (j + 1) * size)
        dot = jnp.dot(
            rows_ref[:, part], weights_ref[part, :], preferred_element_type=jnp.float32
        )
        if j == 0:
            total_ref[:, :units] = dot
        else:
            total_ref[:, :units] += dot
    hidden_ref[...] = jnp.maximum(total_ref[:, :units], 0.0).astype(jnp.bfloat16)
    for j in range(cuts):
        for copy in copies[cuts + j]:
            copy.wait()
        size = units // cuts
        part = slice(j * size, (j + 1) * size)
        for i in range(panels):
            start = width + i * units + j * size
            columns = slice(i * units, (i + 1) * units)
            dot = jnp.dot(
                hidden_ref[:, part],
                weights_ref[start : start + size, :],
                preferred_element_type=jnp.float32,
            )
            if j > 0:
                dot += total_ref[:, columns]
            if j < cuts - 1:
                total_ref[:, columns] = dot
            else:
                out = (dot * gate).astype(jnp.bfloat16)
                keep_ref[:, columns] = out[:half]
                send_ref[:, columns] = out[half:]


def load_ffn(kept, sent, w_first, w_second, experts, expert):
    width, units = w_first.shape
    half, cuts = kept.shape[0], 4
    out = jax.ShapeDtypeStruct((half, width), jnp.bfloat16)
    return pl.pallas_call(
        functools.partial(load_ffn_kernel, experts, cuts),
        out_shape=(out, out, pltpu.VMEM((2 * width, units), w_first.dtype)),
        in_specs=[pl.BlockSpec(memory_space=pltpu.SMEM), VMEM, VMEM, ANY, ANY],
        out_specs=(VMEM, VMEM, VMEM),
        scratch_shapes=[
            pltpu.VMEM((2 * half, width + LANES), jnp.bfloat16),
            pltpu.VMEM((2 * half, units), jnp.bfloat16),
            pltpu.VMEM((2 * half, width), jnp.float32),
            pltpu.SemaphoreType.DMA((1 + width // units, cuts)),
        ],
        compiler_params=pltpu.CompilerParams(vmem_limit_bytes=16 * 1024 * 1024),
        cost_estimate=pl.CostEstimate(
            flops=8 * half * width * units, bytes_accessed=4 * width * units, transcendentals=0
        ),
        name="load_ffn",
    )(expert, kept, sent, in_hbm(w_first), in_hbm(w_second))


def ffn_kernel(experts, pieces, skipped, expert_ref, *refs):
    kept, sent = refs[:pieces], refs[pieces : 2 * pieces]
    weights = refs[2 * pieces]
    keep_ref, send_ref, rows_ref, hidden_ref = refs[2 * pieces + 1 + skipped :]
    width, units = keep_ref.shape[1], weights.shape[1]
    at = 0
    for ref in kept + sent:
        rows_ref[at : at + ref.shape[0], :] = ref[...]
        at += ref.shape[0]
    half = at // 2
    gate = gate_column(experts, expert_ref, rows_ref[:, width:])
    step = 256
    for j in range(0, units, step):
        dot = jnp.dot(
            rows_ref[:, :width], weights[:width, j : j + step], preferred_element_type=jnp.float32
        )
        hidden_ref[:, j : j + step] = jnp.maximum(dot, 0.0).astype(jnp.bfloat16)
    for j in range(0, width, step):
        start, column = width + j // units * units, j % units
        dot = jnp.dot(
            hidden_ref[...],
            weights[start : start + units, column : column + step],
            preferred_element_type=jnp.float32,
        )
        out = (dot * gate).astype(jnp.bfloat16)
        send_ref[:, j : j + step] = out[half:]
        keep_ref[:, j : j + step] = out[:half]


def ffn(kept, sent, weights, experts, expert, behind):
    width, units = weights.shape[0] // 2, weights.shape[1]
    half = sum(a.shape[0] for a in kept)
    out = jax.ShapeDtypeStruct((half, width), jnp.bfloat16)
    count = len(kept)
    return pl.pallas_call(
        functools.partial(ffn_kernel, experts, count, len(behind)),
        out_shape=(out, out),
        in_specs=[pl.BlockSpec(memory_space=pltpu.SMEM)]
        + [VMEM] * (2 * count + 1)
        + [ANY] * len(behind),
        out_specs=(VMEM, VMEM),
        scratch_shapes=[
            pltpu.VMEM((2 * half, width + LANES), jnp.bfloat16),
            pltpu.VMEM((2 * half, units), jnp.bfloat16),
        ],
        compiler_params=pltpu.CompilerParams(vmem_limit_bytes=16 * 1024 * 1024),
        cost_estimate=pl.CostEstimate(
            flops=8 * half * width * units, bytes_accessed=4 * width * units, transcendentals=0
        ),
        name="ffn",
    )(expert, *kept, *sent, in_vmem(weights), *behind)


def swap(array, axis, distance):
    pairs = [(i, i ^ distance) for i in range(lax.axis_size(axis))]
    return lax.ppermute(array, axis, pairs)


def add(*arrays):
    return sum(a.astype(jnp.float32) for a in arrays)


def dense_body(tokens, routing, gates, ln_gain, w_in, w_out):
    rows = tokens.shape[0]
    experts = lax.axis_size("expert")
    core_bit, chip_bit = 1, 2
    expert = lax.axis_index("expert").reshape(1)

    def run(kept, behind=()):
        sent = swap(kept, "dp", core_bit)
        keep, send = ffn([kept], [sent], weights, experts, expert, behind)
        return keep, swap(send, "dp", core_bit)

    def far_sum(pair, i, count):
        at = slice((count + i) * rows, (count + i + 1) * rows)
        return add(*[a[at] for a in pair]).astype(jnp.bfloat16)

    def near_sum(pair, far, i):
        at = slice(i * rows, (i + 1) * rows)
        return add(*[a[at] for a in pair], swap(far, "dp", chip_bit))

    own = norm_and_pack(tokens, routing, gates, ln_gain, experts)
    across0 = swap(own, "dp", chip_bit)
    lane3, lane1 = swap(own, "expert", 3), swap(own, "expert", 1)
    lane31 = join([lane3, lane1], [across0])
    across31 = swap(lane31, "dp", chip_bit)
    lane2 = swap(join([own], [lane31]), "expert", 2)
    kept0 = join([own, across0], [lane31])
    keep0, send0, weights = load_ffn(
        kept0, swap(kept0, "dp", core_bit), w_in[0], w_out[0], experts, expert
    )
    pair0 = keep0, swap(send0, "dp", core_bit)
    pair31 = run(join([lane31, across31], [pair0[0], lane2]))
    across2 = swap(lane2, "dp", chip_bit)
    kept2 = join([lane2, across2], [pair31[0]], DEAR)
    far3 = join([far_sum(pair31, 0, 2)], [kept2])
    pair2 = run(kept2, [far3])
    far2 = far_sum(pair2, 0, 1)
    far1 = join([far_sum(pair31, 1, 2)], [far2])
    far0 = join([far_sum(pair0, 0, 1)], [far2])
    near3 = near_sum(pair31, far3, 0).astype(jnp.bfloat16)
    near2 = near_sum(pair2, far2, 0).astype(jnp.bfloat16)
    near1 = near_sum(pair31, far1, 1).astype(jnp.bfloat16)
    near0 = near_sum(pair0, far0, 0)
    return add(
        tokens,
        near0,
        swap(near3, "expert", 3),
        swap(near1, "expert", 1),
        swap(near2, "expert", 2),
    ).astype(jnp.bfloat16)


def layer_norm(tokens, ln_gain):
    values = tokens.astype(jnp.float32)
    center = values - jnp.mean(values, axis=1, keepdims=True)
    variance = jnp.mean(center * center, axis=1, keepdims=True)
    return (center * lax.rsqrt(variance + 1e-05) * ln_gain).astype(jnp.bfloat16)


def slot_index(routing, experts, capacity):
    flat_ids = routing.reshape(-1)
    onehot = (flat_ids[:, None] == jnp.arange(experts, dtype=jnp.int32)[None, :]).astype(jnp.int32)
    rank_run = jnp.cumsum(onehot, axis=0) - 1
    own_rank = jnp.sum(onehot * rank_run, axis=1)
    return flat_ids * capacity + own_rank


def pack_slots(normed, routing, experts, capacity):
    slots = slot_index(routing, experts, capacity)
    picker = (slots[None, :] == jnp.arange(experts * capacity, dtype=jnp.int32)[:, None]).astype(
        jnp.bfloat16
    )
    picker = picker.reshape(experts * capacity, normed.shape[0], routing.shape[1]).sum(axis=2)
    outgoing = jnp.dot(picker, normed, preferred_element_type=jnp.float32).astype(jnp.bfloat16)
    return outgoing.reshape(experts, capacity, normed.shape[1])


def run_experts(block_in, w_first, w_second):
    dims_in = block_in.shape
    row_mat = block_in.reshape(-1, dims_in[-1])
    hidden = jnp.maximum(jnp.dot(row_mat, w_first, preferred_element_type=jnp.float32), 0.0).astype(
        jnp.bfloat16
    )
    product = jnp.dot(hidden, w_second, preferred_element_type=jnp.float32).astype(jnp.bfloat16)
    return product.reshape(dims_in)


def slot_body(tokens, routing, gates, ln_gain, w_in, w_out):
    rows_dev = tokens.shape[0]
    feature_dim = tokens.shape[1]
    top_count = routing.shape[1]
    experts = lax.axis_size("expert")
    dp_size = lax.axis_size("dp")
    capacity = max(2, min(rows_dev, 2 * rows_dev * top_count // experts))
    w_first = w_in[0]
    w_second = w_out[0]
    normed = layer_norm(tokens, ln_gain)
    own_slots = slot_index(routing, experts, capacity)
    all_normed, all_routes = (
        lax.all_gather(normed, "dp", axis=0, tiled=True),
        lax.all_gather(routing, "dp", axis=0, tiled=True),
    )

    def pack_member(member_rows, member_routes):
        return pack_slots(member_rows, member_routes, experts, capacity)

    packed = jax.vmap(pack_member)(
        all_normed.reshape(dp_size, rows_dev, feature_dim),
        all_routes.reshape(dp_size, rows_dev, top_count),
    )
    partials = run_experts(
        lax.all_to_all(packed, "expert", split_axis=1, concat_axis=1, tiled=True), w_first, w_second
    )
    returned = lax.all_to_all(
        lax.all_to_all(partials, "expert", split_axis=1, concat_axis=1, tiled=True),
        "dp",
        split_axis=0,
        concat_axis=0,
        tiled=True,
    )
    block_total = returned.astype(jnp.float32).sum(axis=0)
    expert_out = block_total.astype(jnp.bfloat16).reshape(experts * capacity, feature_dim)
    expert_out = lax.optimization_barrier(expert_out)
    picker = (
        own_slots[:, None] == jnp.arange(experts * capacity, dtype=jnp.int32)[None, :]
    ).astype(jnp.bfloat16)
    values = jnp.dot(picker, expert_out, preferred_element_type=jnp.float32)
    weighted = values.reshape(rows_dev, top_count, feature_dim) * gates[:, :, None]
    return (tokens.astype(jnp.float32) + weighted.sum(axis=1)).astype(jnp.bfloat16)


def body(tokens, routing, gates, ln_gain, w_in, w_out):
    rows_dev = tokens.shape[0]
    experts = lax.axis_size("expert")
    capacity = max(2, min(rows_dev, 2 * rows_dev * routing.shape[1] // experts))
    if capacity == rows_dev and experts == 4 and lax.axis_size("dp") == 4:
        return dense_body(tokens, routing, gates, ln_gain, w_in, w_out)
    return slot_body(tokens, routing, gates, ln_gain, w_in, w_out)


def solution(mesh):
    placed = (
        P(("groups", "expert", "dp"), None),
        P(("groups", "expert", "dp"), None),
        P(("groups", "expert", "dp"), None),
        P(),
        P("expert", None, "dp"),
        P("expert", "dp", None),
    )
    return jax.shard_map(
        body,
        mesh=mesh,
        in_specs=placed,
        out_specs=P(("groups", "expert", "dp"), None),
        check_vma=False,
    )
```

```python
import functools

import jax
import jax.numpy as jnp
from jax import lax
from jax.experimental import pallas as pl
from jax.experimental.pallas import tpu as pltpu
from jax.sharding import PartitionSpec as P

LANES = 128
GATE_TERMS = 3
VMEM = pl.BlockSpec(memory_space=pltpu.VMEM)
SMALL = pltpu.CompilerParams(vmem_limit_bytes=4 * 1024 * 1024)
CHEAP = pl.CostEstimate(flops=1, bytes_accessed=1, transcendentals=0)
DEAR = pl.CostEstimate(flops=10**10, bytes_accessed=1, transcendentals=0)
ANY = pl.BlockSpec(memory_space=pl.ANY)


def in_hbm(array):
    return pltpu.with_memory_space_constraint(array, pltpu.HBM)


def in_vmem(array):
    return pltpu.with_memory_space_constraint(array, pltpu.VMEM)


def norm_kernel(experts, *refs):
    sources, out_ref, targets, sems = refs[:4], refs[4], refs[5:9], refs[9]
    copies = [
        pltpu.make_async_copy(source, target, sems.at[i])
        for i, (source, target) in enumerate(zip(sources, targets))
    ]
    for copy in copies:
        copy.start()
    for copy in copies:
        copy.wait()
    tokens_ref, routing_ref, gates_ref, gain_ref = targets
    width = tokens_ref.shape[1]
    values = tokens_ref[...].astype(jnp.float32)
    center = values - jnp.mean(values, axis=1, keepdims=True)
    variance = jnp.mean(center * center, axis=1, keepdims=True)
    normed = center * lax.rsqrt(variance + 1e-05) * gain_ref[...]
    out_ref[:, :width] = normed.astype(jnp.bfloat16)
    lane = lax.broadcasted_iota(jnp.int32, (LANES, tokens_ref.shape[0]), 0)
    expert = lax.rem(lane, experts)
    term = lax.div(lane, experts)
    gate = jnp.zeros(lane.shape, jnp.float32)
    for k in range(routing_ref.shape[0]):
        gate += jnp.where(routing_ref[k : k + 1, :] == expert, gates_ref[k : k + 1, :], 0.0)
    rest = gate
    packed = jnp.zeros(lane.shape, jnp.float32)
    for i in range(GATE_TERMS):
        part = rest.astype(jnp.bfloat16).astype(jnp.float32)
        packed = jnp.where(term == i, part, packed)
        rest = rest - part
    out_ref[:, width:] = packed.T.astype(jnp.bfloat16)


def norm_and_pack(tokens, routing, gates, ln_gain, experts):
    rows, width = tokens.shape
    arrays = (tokens, routing.T, gates.T, ln_gain.reshape(1, width))
    return pl.pallas_call(
        functools.partial(norm_kernel, experts),
        out_shape=pltpu.VMEM((rows, width + LANES), jnp.bfloat16),
        in_specs=[ANY] * 4,
        out_specs=VMEM,
        scratch_shapes=[pltpu.VMEM(a.shape, a.dtype) for a in arrays]
        + [pltpu.SemaphoreType.DMA((4,))],
        compiler_params=SMALL,
        cost_estimate=CHEAP,
        name="norm",
    )(*[in_hbm(a) for a in arrays])


def join_kernel(pieces, *refs):
    at = 0
    for ref in refs[:pieces]:
        refs[-1][at : at + ref.shape[0], :] = ref[...]
        at += ref.shape[0]


def join(arrays, behind=(), cost=CHEAP):
    rows, width = sum(a.shape[0] for a in arrays), arrays[0].shape[1]
    return pl.pallas_call(
        functools.partial(join_kernel, len(arrays)),
        out_shape=pltpu.VMEM((rows, width), arrays[0].dtype),
        in_specs=[VMEM] * len(arrays) + [ANY] * len(behind),
        out_specs=VMEM,
        compiler_params=SMALL,
        cost_estimate=cost,
        name="join",
    )(*arrays, *behind)


def mark_kernel(*refs):
    refs[-1][...] = jnp.zeros_like(refs[-1])


def mark(behind, cost):
    return pl.pallas_call(
        mark_kernel,
        out_shape=pltpu.VMEM((8, LANES), jnp.float32),
        in_specs=[ANY] * len(behind),
        out_specs=VMEM,
        compiler_params=SMALL,
        cost_estimate=cost,
        name="mark",
    )(*behind)


def part_kernel(start, count, *refs):
    rows = refs[-1].shape[0]
    total = jnp.zeros(refs[-1].shape, jnp.float32)
    for ref in refs[:count]:
        at = start if ref.shape[0] > rows else 0
        total += ref[at : at + rows, :].astype(jnp.float32)
    refs[-1][...] = total.astype(refs[-1].dtype)


def part_sum(arrays, start, rows, behind=(), cost=CHEAP):
    return pl.pallas_call(
        functools.partial(part_kernel, start, len(arrays)),
        out_shape=pltpu.VMEM((rows, arrays[0].shape[1]), jnp.bfloat16),
        in_specs=[VMEM] * len(arrays) + [ANY] * len(behind),
        out_specs=VMEM,
        compiler_params=SMALL,
        cost_estimate=cost,
        name="part",
    )(*arrays, *behind)


def sum_kernel(*refs):
    total = refs[0][...].astype(jnp.float32)
    for ref in refs[1:-1]:
        total += ref[...].astype(jnp.float32)
    refs[-1][...] = total


def sum_arrays(arrays, cost):
    return pl.pallas_call(
        sum_kernel,
        out_shape=pltpu.VMEM(arrays[0].shape, jnp.float32),
        in_specs=[VMEM] * len(arrays),
        out_specs=VMEM,
        compiler_params=SMALL,
        cost_estimate=cost,
        name="sum",
    )(*arrays)


def gate_column(experts, expert_ref, tail):
    lane = lax.broadcasted_iota(jnp.int32, tail.shape, 1)
    chosen = (lax.rem(lane, experts) == expert_ref[0]) & (lane < GATE_TERMS * experts)
    return jnp.sum(jnp.where(chosen, tail.astype(jnp.float32), 0.0), axis=1, keepdims=True)


def load_ffn_kernel(
    experts, cuts, skipped, expert_ref, kept_ref, sent_ref, first_ref, second_ref, *refs
):
    keep_ref, send_ref, weights_ref, rows_ref, hidden_ref, total_ref, sems = refs[skipped:]
    width, units = first_ref.shape
    copies = []
    for j in range(cuts):
        size = width // cuts
        part = pl.ds(j * size, size)
        copies.append(
            [pltpu.make_async_copy(first_ref.at[part], weights_ref.at[part], sems.at[0, j])]
        )
    panels = second_ref.shape[1] // units
    for j in range(cuts):
        size = units // cuts
        copies.append(
            [
                pltpu.make_async_copy(
                    second_ref.at[pl.ds(j * size, size), pl.ds(i * units, units)],
                    weights_ref.at[pl.ds(width + i * units + j * size, size)],
                    sems.at[1 + i, j],
                )
                for i in range(panels)
            ]
        )
    for group in copies:
        for copy in group:
            copy.start()
    half = kept_ref.shape[0]
    rows_ref[:half, :] = kept_ref[...]
    rows_ref[half:, :] = sent_ref[...]
    gate = gate_column(experts, expert_ref, rows_ref[:, width:])
    for j in range(cuts):
        for copy in copies[j]:
            copy.wait()
        size = width // cuts
        part = slice(j * size, (j + 1) * size)
        dot = jnp.dot(
            rows_ref[:, part], weights_ref[part, :], preferred_element_type=jnp.float32
        )
        if j == 0:
            total_ref[:, :units] = dot
        else:
            total_ref[:, :units] += dot
    hidden_ref[...] = jnp.maximum(total_ref[:, :units], 0.0).astype(jnp.bfloat16)
    for j in range(cuts):
        for copy in copies[cuts + j]:
            copy.wait()
        size = units // cuts
        part = slice(j * size, (j + 1) * size)
        for i in range(panels):
            start = width + i * units + j * size
            columns = slice(i * units, (i + 1) * units)
            dot = jnp.dot(
                hidden_ref[:, part],
                weights_ref[start : start + size, :],
                preferred_element_type=jnp.float32,
            )
            if j > 0:
                dot += total_ref[:, columns]
            if j < cuts - 1:
                total_ref[:, columns] = dot
            else:
                out = (dot * gate).astype(jnp.bfloat16)
                keep_ref[:, columns] = out[:half]
                send_ref[:, columns] = out[half:]


def load_ffn(kept, sent, w_first, w_second, experts, expert, behind):
    width, units = w_first.shape
    half, cuts = kept.shape[0], 4
    out = jax.ShapeDtypeStruct((half, width), jnp.bfloat16)
    return pl.pallas_call(
        functools.partial(load_ffn_kernel, experts, cuts, len(behind)),
        out_shape=(out, out, pltpu.VMEM((2 * width, units), w_first.dtype)),
        in_specs=[pl.BlockSpec(memory_space=pltpu.SMEM), VMEM, VMEM] + [ANY] * (2 + len(behind)),
        out_specs=(VMEM, VMEM, VMEM),
        scratch_shapes=[
            pltpu.VMEM((2 * half, width + LANES), jnp.bfloat16),
            pltpu.VMEM((2 * half, units), jnp.bfloat16),
            pltpu.VMEM((2 * half, width), jnp.float32),
            pltpu.SemaphoreType.DMA((1 + width // units, cuts)),
        ],
        compiler_params=pltpu.CompilerParams(vmem_limit_bytes=16 * 1024 * 1024),
        cost_estimate=DEAR,
        name="load_ffn",
    )(expert, kept, sent, in_hbm(w_first), in_hbm(w_second), *behind)


def ffn_kernel(experts, pieces, skipped, expert_ref, *refs):
    kept, sent = refs[:pieces], refs[pieces : 2 * pieces]
    weights = refs[2 * pieces]
    keep_ref, send_ref, rows_ref, hidden_ref = refs[2 * pieces + 1 + skipped :]
    width, units = keep_ref.shape[1], weights.shape[1]
    at = 0
    for ref in kept + sent:
        rows_ref[at : at + ref.shape[0], :] = ref[...]
        at += ref.shape[0]
    half = at // 2
    gate = gate_column(experts, expert_ref, rows_ref[:, width:])
    step = 256
    for j in range(0, units, step):
        dot = jnp.dot(
            rows_ref[:, :width], weights[:width, j : j + step], preferred_element_type=jnp.float32
        )
        hidden_ref[:, j : j + step] = jnp.maximum(dot, 0.0).astype(jnp.bfloat16)
    for j in range(0, width, step):
        start, column = width + j // units * units, j % units
        dot = jnp.dot(
            hidden_ref[...],
            weights[start : start + units, column : column + step],
            preferred_element_type=jnp.float32,
        )
        out = (dot * gate).astype(jnp.bfloat16)
        send_ref[:, j : j + step] = out[half:]
        keep_ref[:, j : j + step] = out[:half]


def ffn(kept, sent, weights, experts, expert, behind):
    width, units = weights.shape[0] // 2, weights.shape[1]
    half = sum(a.shape[0] for a in kept)
    out = jax.ShapeDtypeStruct((half, width), jnp.bfloat16)
    count = len(kept)
    return pl.pallas_call(
        functools.partial(ffn_kernel, experts, count, len(behind)),
        out_shape=(out, out),
        in_specs=[pl.BlockSpec(memory_space=pltpu.SMEM)]
        + [VMEM] * (2 * count + 1)
        + [ANY] * len(behind),
        out_specs=(VMEM, VMEM),
        scratch_shapes=[
            pltpu.VMEM((2 * half, width + LANES), jnp.bfloat16),
            pltpu.VMEM((2 * half, units), jnp.bfloat16),
        ],
        compiler_params=pltpu.CompilerParams(vmem_limit_bytes=16 * 1024 * 1024),
        cost_estimate=pl.CostEstimate(
            flops=8 * half * width * units, bytes_accessed=4 * width * units, transcendentals=0
        ),
        name="ffn",
    )(expert, *kept, *sent, in_vmem(weights), *behind)


def swap(array, axis, distance):
    pairs = [(i, i ^ distance) for i in range(lax.axis_size(axis))]
    return lax.ppermute(array, axis, pairs)


def add(*arrays):
    return sum(a.astype(jnp.float32) for a in arrays)


def dense_body(tokens, routing, gates, ln_gain, w_in, w_out):
    rows = tokens.shape[0]
    experts = lax.axis_size("expert")
    core_bit, chip_bit = 1, 2
    expert = lax.axis_index("expert").reshape(1)

    def run(kept, behind=()):
        sent = swap(kept, "dp", core_bit)
        keep, send = ffn([kept], [sent], weights, experts, expert, behind)
        return keep, swap(send, "dp", core_bit)

    own = norm_and_pack(tokens, routing, gates, ln_gain, experts)
    across0 = swap(own, "dp", chip_bit)
    lane3, lane1 = swap(own, "expert", 3), swap(own, "expert", 1)
    lane31 = join([lane3, lane1])
    across31 = swap(lane31, "dp", chip_bit)
    lane2 = swap(own, "expert", 2)
    kept0 = join([own, across0], [lane31])
    keep0, send0, weights = load_ffn(
        kept0,
        swap(kept0, "dp", core_bit),
        w_in[0],
        w_out[0],
        experts,
        expert,
        [mark([lane2], DEAR)],
    )
    pair0 = keep0, swap(send0, "dp", core_bit)
    across2 = swap(lane2, "dp", chip_bit)
    kept31 = join([lane31, across31], [keep0])
    pair31 = run(kept31, [mark([across2, kept31], DEAR)])
    pair2 = run(join([lane2, across2], [kept31]), [pair31[0]])
    far3 = part_sum(pair31, 2 * rows, rows, [pair2[0]])
    far2 = part_sum(pair2, rows, rows)
    far1 = part_sum(pair31, 3 * rows, rows, [far2])
    far0 = part_sum(pair0, rows, rows, [far2])
    near3 = part_sum([*pair31, swap(far3, "dp", chip_bit)], 0, rows)
    near2 = part_sum([*pair2, swap(far2, "dp", chip_bit)], 0, rows)
    near1 = part_sum([*pair31, swap(far1, "dp", chip_bit)], rows, rows)
    near0 = add(*[a[:rows] for a in pair0], swap(far0, "dp", chip_bit))
    total = sum_arrays([tokens, swap(near3, "expert", 3)], CHEAP)
    total = sum_arrays([total, swap(near2, "expert", 2)], CHEAP)
    return add(total, near0, swap(near1, "expert", 1)).astype(jnp.bfloat16)


def layer_norm(tokens, ln_gain):
    values = tokens.astype(jnp.float32)
    center = values - jnp.mean(values, axis=1, keepdims=True)
    variance = jnp.mean(center * center, axis=1, keepdims=True)
    return (center * lax.rsqrt(variance + 1e-05) * ln_gain).astype(jnp.bfloat16)


def slot_index(routing, experts, capacity):
    flat_ids = routing.reshape(-1)
    onehot = (flat_ids[:, None] == jnp.arange(experts, dtype=jnp.int32)[None, :]).astype(jnp.int32)
    rank_run = jnp.cumsum(onehot, axis=0) - 1
    own_rank = jnp.sum(onehot * rank_run, axis=1)
    return flat_ids * capacity + own_rank


def pack_slots(normed, routing, experts, capacity):
    slots = slot_index(routing, experts, capacity)
    picker = (slots[None, :] == jnp.arange(experts * capacity, dtype=jnp.int32)[:, None]).astype(
        jnp.bfloat16
    )
    picker = picker.reshape(experts * capacity, normed.shape[0], routing.shape[1]).sum(axis=2)
    outgoing = jnp.dot(picker, normed, preferred_element_type=jnp.float32).astype(jnp.bfloat16)
    return outgoing.reshape(experts, capacity, normed.shape[1])


def run_experts(block_in, w_first, w_second):
    dims_in = block_in.shape
    row_mat = block_in.reshape(-1, dims_in[-1])
    hidden = jnp.maximum(jnp.dot(row_mat, w_first, preferred_element_type=jnp.float32), 0.0).astype(
        jnp.bfloat16
    )
    product = jnp.dot(hidden, w_second, preferred_element_type=jnp.float32).astype(jnp.bfloat16)
    return product.reshape(dims_in)


def slot_body(tokens, routing, gates, ln_gain, w_in, w_out):
    rows_dev = tokens.shape[0]
    feature_dim = tokens.shape[1]
    top_count = routing.shape[1]
    experts = lax.axis_size("expert")
    dp_size = lax.axis_size("dp")
    capacity = max(2, min(rows_dev, 2 * rows_dev * top_count // experts))
    w_first = w_in[0]
    w_second = w_out[0]
    normed = layer_norm(tokens, ln_gain)
    own_slots = slot_index(routing, experts, capacity)
    all_normed, all_routes = (
        lax.all_gather(normed, "dp", axis=0, tiled=True),
        lax.all_gather(routing, "dp", axis=0, tiled=True),
    )

    def pack_member(member_rows, member_routes):
        return pack_slots(member_rows, member_routes, experts, capacity)

    packed = jax.vmap(pack_member)(
        all_normed.reshape(dp_size, rows_dev, feature_dim),
        all_routes.reshape(dp_size, rows_dev, top_count),
    )
    partials = run_experts(
        lax.all_to_all(packed, "expert", split_axis=1, concat_axis=1, tiled=True), w_first, w_second
    )
    returned = lax.all_to_all(
        lax.all_to_all(partials, "expert", split_axis=1, concat_axis=1, tiled=True),
        "dp",
        split_axis=0,
        concat_axis=0,
        tiled=True,
    )
    block_total = returned.astype(jnp.float32).sum(axis=0)
    expert_out = block_total.astype(jnp.bfloat16).reshape(experts * capacity, feature_dim)
    expert_out = lax.optimization_barrier(expert_out)
    picker = (
        own_slots[:, None] == jnp.arange(experts * capacity, dtype=jnp.int32)[None, :]
    ).astype(jnp.bfloat16)
    values = jnp.dot(picker, expert_out, preferred_element_type=jnp.float32)
    weighted = values.reshape(rows_dev, top_count, feature_dim) * gates[:, :, None]
    return (tokens.astype(jnp.float32) + weighted.sum(axis=1)).astype(jnp.bfloat16)


def body(tokens, routing, gates, ln_gain, w_in, w_out):
    rows_dev = tokens.shape[0]
    experts = lax.axis_size("expert")
    capacity = max(2, min(rows_dev, 2 * rows_dev * routing.shape[1] // experts))
    if capacity == rows_dev and experts == 4 and lax.axis_size("dp") == 4:
        return dense_body(tokens, routing, gates, ln_gain, w_in, w_out)
    return slot_body(tokens, routing, gates, ln_gain, w_in, w_out)


def solution(mesh):
    placed = (
        P(("groups", "expert", "dp"), None),
        P(("groups", "expert", "dp"), None),
        P(("groups", "expert", "dp"), None),
        P(),
        P("expert", None, "dp"),
        P("expert", "dp", None),
    )
    return jax.shard_map(
        body,
        mesh=mesh,
        in_specs=placed,
        out_specs=P(("groups", "expert", "dp"), None),
        check_vma=False,
    )
```

```python
import functools

import jax
import jax.numpy as jnp
from jax import lax
from jax.experimental import pallas as pl
from jax.experimental.pallas import tpu as pltpu
from jax.sharding import PartitionSpec as P

LANES = 128
GATE_TERMS = 3
VMEM = pl.BlockSpec(memory_space=pltpu.VMEM)
SMALL = pltpu.CompilerParams(vmem_limit_bytes=4 * 1024 * 1024)
CHEAP = pl.CostEstimate(flops=1, bytes_accessed=1, transcendentals=0)
DEAR = pl.CostEstimate(flops=10**10, bytes_accessed=1, transcendentals=0)
SOME = pl.CostEstimate(flops=2*10**9, bytes_accessed=1, transcendentals=0)
ANY = pl.BlockSpec(memory_space=pl.ANY)


def in_hbm(array):
    return pltpu.with_memory_space_constraint(array, pltpu.HBM)


def in_vmem(array):
    return pltpu.with_memory_space_constraint(array, pltpu.VMEM)


def norm_kernel(experts, *refs):
    sources, out_ref, targets, sems = refs[:4], refs[4], refs[5:9], refs[9]
    copies = [
        pltpu.make_async_copy(source, target, sems.at[i])
        for i, (source, target) in enumerate(zip(sources, targets))
    ]
    for copy in copies:
        copy.start()
    for copy in copies:
        copy.wait()
    tokens_ref, routing_ref, gates_ref, gain_ref = targets
    width = tokens_ref.shape[1]
    values = tokens_ref[...].astype(jnp.float32)
    center = values - jnp.mean(values, axis=1, keepdims=True)
    variance = jnp.mean(center * center, axis=1, keepdims=True)
    normed = center * lax.rsqrt(variance + 1e-05) * gain_ref[...]
    out_ref[:, :width] = normed.astype(jnp.bfloat16)
    lane = lax.broadcasted_iota(jnp.int32, (LANES, tokens_ref.shape[0]), 0)
    expert = lax.rem(lane, experts)
    term = lax.div(lane, experts)
    gate = jnp.zeros(lane.shape, jnp.float32)
    for k in range(routing_ref.shape[0]):
        gate += jnp.where(routing_ref[k : k + 1, :] == expert, gates_ref[k : k + 1, :], 0.0)
    rest = gate
    packed = jnp.zeros(lane.shape, jnp.float32)
    for i in range(GATE_TERMS):
        part = rest.astype(jnp.bfloat16).astype(jnp.float32)
        packed = jnp.where(term == i, part, packed)
        rest = rest - part
    out_ref[:, width:] = packed.T.astype(jnp.bfloat16)


def norm_and_pack(tokens, routing, gates, ln_gain, experts):
    rows, width = tokens.shape
    arrays = (tokens, routing.T, gates.T, ln_gain.reshape(1, width))
    return pl.pallas_call(
        functools.partial(norm_kernel, experts),
        out_shape=pltpu.VMEM((rows, width + LANES), jnp.bfloat16),
        in_specs=[ANY] * 4,
        out_specs=VMEM,
        scratch_shapes=[pltpu.VMEM(a.shape, a.dtype) for a in arrays]
        + [pltpu.SemaphoreType.DMA((4,))],
        compiler_params=SMALL,
        cost_estimate=CHEAP,
        name="norm",
    )(*[in_hbm(a) for a in arrays])


def join_kernel(pieces, *refs):
    at = 0
    for ref, (start, size) in zip(refs, pieces):
        refs[-1][at : at + size, :] = ref[start : start + size, :]
        at += size


def join(arrays, behind=(), pieces=None, cost=CHEAP):
    pieces = pieces or [(0, a.shape[0]) for a in arrays]
    rows, width = sum(size for _, size in pieces), arrays[0].shape[1]
    return pl.pallas_call(
        functools.partial(join_kernel, pieces),
        out_shape=pltpu.VMEM((rows, width), arrays[0].dtype),
        in_specs=[VMEM] * len(arrays) + [ANY] * len(behind),
        out_specs=VMEM,
        compiler_params=SMALL,
        cost_estimate=cost,
        name="join",
    )(*arrays, *behind)


def mark_kernel(*refs):
    refs[-1][...] = jnp.zeros_like(refs[-1])


def mark(behind, cost):
    return pl.pallas_call(
        mark_kernel,
        out_shape=pltpu.VMEM((8, LANES), jnp.float32),
        in_specs=[ANY] * len(behind),
        out_specs=VMEM,
        compiler_params=SMALL,
        cost_estimate=cost,
        name="mark",
    )(*behind)


def part_kernel(start, count, *refs):
    rows = refs[-1].shape[0]
    total = jnp.zeros(refs[-1].shape, jnp.float32)
    for ref in refs[:count]:
        at = start if ref.shape[0] > rows else 0
        total += ref[at : at + rows, :].astype(jnp.float32)
    refs[-1][...] = total.astype(refs[-1].dtype)


def part_sum(arrays, start, rows, behind=(), cost=CHEAP):
    return pl.pallas_call(
        functools.partial(part_kernel, start, len(arrays)),
        out_shape=pltpu.VMEM((rows, arrays[0].shape[1]), jnp.bfloat16),
        in_specs=[VMEM] * len(arrays) + [ANY] * len(behind),
        out_specs=VMEM,
        compiler_params=SMALL,
        cost_estimate=cost,
        name="part",
    )(*arrays, *behind)


def sum_kernel(*refs):
    total = refs[0][...].astype(jnp.float32)
    for ref in refs[1:-1]:
        total += ref[...].astype(jnp.float32)
    refs[-1][...] = total


def sum_arrays(arrays, cost):
    return pl.pallas_call(
        sum_kernel,
        out_shape=pltpu.VMEM(arrays[0].shape, jnp.float32),
        in_specs=[VMEM] * len(arrays),
        out_specs=VMEM,
        compiler_params=SMALL,
        cost_estimate=cost,
        name="sum",
    )(*arrays)


def gate_column(experts, expert_ref, tail):
    lane = lax.broadcasted_iota(jnp.int32, tail.shape, 1)
    chosen = (lax.rem(lane, experts) == expert_ref[0]) & (lane < GATE_TERMS * experts)
    return jnp.sum(jnp.where(chosen, tail.astype(jnp.float32), 0.0), axis=1, keepdims=True)


def load_ffn_kernel(
    experts, cuts, skipped, expert_ref, kept_ref, first_ref, second_ref, *refs
):
    keep_ref, weights_ref, rows_ref, hidden_ref, total_ref, sems = refs[skipped:]
    width, units = first_ref.shape
    copies = []
    for j in range(cuts):
        size = width // cuts
        part = pl.ds(j * size, size)
        copies.append(
            [pltpu.make_async_copy(first_ref.at[part], weights_ref.at[part], sems.at[0, j])]
        )
    panels = second_ref.shape[1] // units
    for j in range(cuts):
        size = units // cuts
        copies.append(
            [
                pltpu.make_async_copy(
                    second_ref.at[pl.ds(j * size, size), pl.ds(i * units, units)],
                    weights_ref.at[pl.ds(width + i * units + j * size, size)],
                    sems.at[1 + i, j],
                )
                for i in range(panels)
            ]
        )
    for group in copies:
        for copy in group:
            copy.start()
    rows_ref[...] = kept_ref[...]
    gate = gate_column(experts, expert_ref, rows_ref[:, width:])
    for j in range(cuts):
        for copy in copies[j]:
            copy.wait()
        size = width // cuts
        part = slice(j * size, (j + 1) * size)
        dot = jnp.dot(
            rows_ref[:, part], weights_ref[part, :], preferred_element_type=jnp.float32
        )
        if j == 0:
            total_ref[:, :units] = dot
        else:
            total_ref[:, :units] += dot
    hidden_ref[...] = jnp.maximum(total_ref[:, :units], 0.0).astype(jnp.bfloat16)
    for j in range(cuts):
        for copy in copies[cuts + j]:
            copy.wait()
        size = units // cuts
        part = slice(j * size, (j + 1) * size)
        for i in range(panels):
            start = width + i * units + j * size
            columns = slice(i * units, (i + 1) * units)
            dot = jnp.dot(
                hidden_ref[:, part],
                weights_ref[start : start + size, :],
                preferred_element_type=jnp.float32,
            )
            if j > 0:
                dot += total_ref[:, columns]
            if j < cuts - 1:
                total_ref[:, columns] = dot
            else:
                out = (dot * gate).astype(jnp.bfloat16)
                keep_ref[:, columns] = out


def load_ffn(kept, w_first, w_second, experts, expert, behind):
    width, units = w_first.shape
    rows, cuts = kept.shape[0], 4
    out = jax.ShapeDtypeStruct((rows, width), jnp.bfloat16)
    return pl.pallas_call(
        functools.partial(load_ffn_kernel, experts, cuts, len(behind)),
        out_shape=(out, pltpu.VMEM((2 * width, units), w_first.dtype)),
        in_specs=[pl.BlockSpec(memory_space=pltpu.SMEM), VMEM] + [ANY] * (2 + len(behind)),
        out_specs=(VMEM, VMEM),
        scratch_shapes=[
            pltpu.VMEM((rows, width + LANES), jnp.bfloat16),
            pltpu.VMEM((rows, units), jnp.bfloat16),
            pltpu.VMEM((rows, width), jnp.float32),
            pltpu.SemaphoreType.DMA((1 + width // units, cuts)),
        ],
        compiler_params=pltpu.CompilerParams(vmem_limit_bytes=16 * 1024 * 1024),
        cost_estimate=CHEAP,
        name="load_ffn",
    )(expert, kept, in_hbm(w_first), in_hbm(w_second), *behind)


def ffn_kernel(experts, kept_count, sent_count, skipped, expert_ref, *refs):
    pieces = kept_count + sent_count
    kept, sent = refs[:kept_count], refs[kept_count:pieces]
    weights = refs[pieces]
    keep_ref, send_ref, rows_ref, hidden_ref = refs[pieces + 1 + skipped :]
    width, units = keep_ref.shape[1], weights.shape[1]
    at = 0
    for ref in kept + sent:
        rows_ref[at : at + ref.shape[0], :] = ref[...]
        at += ref.shape[0]
    half = keep_ref.shape[0]
    gate = gate_column(experts, expert_ref, rows_ref[:, width:])
    step = 256
    for j in range(0, units, step):
        dot = jnp.dot(
            rows_ref[:, :width], weights[:width, j : j + step], preferred_element_type=jnp.float32
        )
        hidden_ref[:, j : j + step] = jnp.maximum(dot, 0.0).astype(jnp.bfloat16)
    for j in range(0, width, step):
        start, column = width + j // units * units, j % units
        dot = jnp.dot(
            hidden_ref[...],
            weights[start : start + units, column : column + step],
            preferred_element_type=jnp.float32,
        )
        out = (dot * gate).astype(jnp.bfloat16)
        send_ref[:, j : j + step] = out[half:]
        keep_ref[:, j : j + step] = out[:half]


def ffn(kept, sent, weights, experts, expert, behind, cost):
    width, units = weights.shape[0] // 2, weights.shape[1]
    half = sum(a.shape[0] for a in kept)
    rest = sum(a.shape[0] for a in sent)
    count = len(kept) + len(sent)
    return pl.pallas_call(
        functools.partial(ffn_kernel, experts, len(kept), len(sent), len(behind)),
        out_shape=(
            jax.ShapeDtypeStruct((half, width), jnp.bfloat16),
            jax.ShapeDtypeStruct((rest, width), jnp.bfloat16),
        ),
        in_specs=[pl.BlockSpec(memory_space=pltpu.SMEM)]
        + [VMEM] * (count + 1)
        + [ANY] * len(behind),
        out_specs=(VMEM, VMEM),
        scratch_shapes=[
            pltpu.VMEM((half + rest, width + LANES), jnp.bfloat16),
            pltpu.VMEM((half + rest, units), jnp.bfloat16),
        ],
        compiler_params=pltpu.CompilerParams(vmem_limit_bytes=16 * 1024 * 1024),
        cost_estimate=pl.CostEstimate(
            flops=4 * (half + rest) * width * units, bytes_accessed=4 * width * units, transcendentals=0
        ),
        name="ffn",
    )(expert, *kept, *sent, in_vmem(weights), *behind)


def swap(array, axis, distance):
    pairs = [(i, i ^ distance) for i in range(lax.axis_size(axis))]
    return lax.ppermute(array, axis, pairs)


def add(*arrays):
    return sum(a.astype(jnp.float32) for a in arrays)


def dense_body(tokens, routing, gates, ln_gain, w_in, w_out):
    rows = tokens.shape[0]
    experts = lax.axis_size("expert")
    core_bit, chip_bit = 1, 2
    expert = lax.axis_index("expert").reshape(1)

    def run(kept, sent, behind=(), cost=CHEAP):
        keep, send = ffn(kept, sent, weights, experts, expert, behind, cost)
        return keep, swap(send, "dp", core_bit)

    def core_swap(array):
        return swap(array, "dp", core_bit)

    own = norm_and_pack(tokens, routing, gates, ln_gain, experts)
    lane3, lane1 = swap(own, "expert", 3), swap(own, "expert", 1)
    across0 = swap(own, "dp", chip_bit)
    lane2 = swap(own, "expert", 2)
    keep0, weights = load_ffn(own, w_in[0], w_out[0], experts, expert, [])
    lane3 = join([lane3], [keep0])
    across3 = swap(lane3, "dp", chip_bit)
    across1, across2 = swap(lane1, "dp", chip_bit), swap(lane2, "dp", chip_bit)
    kept0 = join([own, across0])
    kept3 = join([lane3, across3], [mark([lane2, mark([lane1, across0], CHEAP)], CHEAP)])
    pair3 = run([kept3], [core_swap(kept3)], [mark([across1, kept3], SOME)])
    far3 = part_sum(pair3, rows, rows, [mark([across2, pair3[0]], SOME)])
    sent0 = join([core_swap(kept0)], [kept3])
    kept2 = join([lane2, across2], [far3, sent0])
    pair2 = run([kept2], [core_swap(kept2)])
    kept1 = join([lane1, across1], [kept2])
    keep1, send10 = ffn(
        [kept1, across0], [core_swap(kept1), sent0], weights, experts, expert, [pair2[0]], CHEAP
    )
    back10 = core_swap(send10)
    near3 = part_sum([*pair3, swap(far3, "dp", chip_bit)], 0, rows, [keep1], DEAR)
    far2 = part_sum(pair2, rows, rows, [near3])
    far1 = part_sum([keep1, back10], rows, rows, [far2])
    near2 = part_sum([*pair2, swap(far2, "dp", chip_bit)], 0, rows, [far1])
    far0 = join([add(keep1[2 * rows :], back10[3 * rows :]).astype(jnp.bfloat16)], [near2])
    near1 = part_sum([keep1, back10, swap(far1, "dp", chip_bit)], 0, rows, [near2])
    near0 = add(keep0, back10[2 * rows : 3 * rows], swap(far0, "dp", chip_bit))
    total = sum_arrays([tokens, swap(near3, "expert", 3)], DEAR)
    return add(total, near0, swap(near1, "expert", 1), swap(near2, "expert", 2)).astype(
        jnp.bfloat16
    )


def layer_norm(tokens, ln_gain):
    values = tokens.astype(jnp.float32)
    center = values - jnp.mean(values, axis=1, keepdims=True)
    variance = jnp.mean(center * center, axis=1, keepdims=True)
    return (center * lax.rsqrt(variance + 1e-05) * ln_gain).astype(jnp.bfloat16)


def slot_index(routing, experts, capacity):
    flat_ids = routing.reshape(-1)
    onehot = (flat_ids[:, None] == jnp.arange(experts, dtype=jnp.int32)[None, :]).astype(jnp.int32)
    rank_run = jnp.cumsum(onehot, axis=0) - 1
    own_rank = jnp.sum(onehot * rank_run, axis=1)
    return flat_ids * capacity + own_rank


def pack_slots(normed, routing, experts, capacity):
    slots = slot_index(routing, experts, capacity)
    picker = (slots[None, :] == jnp.arange(experts * capacity, dtype=jnp.int32)[:, None]).astype(
        jnp.bfloat16
    )
    picker = picker.reshape(experts * capacity, normed.shape[0], routing.shape[1]).sum(axis=2)
    outgoing = jnp.dot(picker, normed, preferred_element_type=jnp.float32).astype(jnp.bfloat16)
    return outgoing.reshape(experts, capacity, normed.shape[1])


def run_experts(block_in, w_first, w_second):
    dims_in = block_in.shape
    row_mat = block_in.reshape(-1, dims_in[-1])
    hidden = jnp.maximum(jnp.dot(row_mat, w_first, preferred_element_type=jnp.float32), 0.0).astype(
        jnp.bfloat16
    )
    product = jnp.dot(hidden, w_second, preferred_element_type=jnp.float32).astype(jnp.bfloat16)
    return product.reshape(dims_in)


def slot_body(tokens, routing, gates, ln_gain, w_in, w_out):
    rows_dev = tokens.shape[0]
    feature_dim = tokens.shape[1]
    top_count = routing.shape[1]
    experts = lax.axis_size("expert")
    dp_size = lax.axis_size("dp")
    capacity = max(2, min(rows_dev, 2 * rows_dev * top_count // experts))
    w_first = w_in[0]
    w_second = w_out[0]
    normed = layer_norm(tokens, ln_gain)
    own_slots = slot_index(routing, experts, capacity)
    all_normed, all_routes = (
        lax.all_gather(normed, "dp", axis=0, tiled=True),
        lax.all_gather(routing, "dp", axis=0, tiled=True),
    )

    def pack_member(member_rows, member_routes):
        return pack_slots(member_rows, member_routes, experts, capacity)

    packed = jax.vmap(pack_member)(
        all_normed.reshape(dp_size, rows_dev, feature_dim),
        all_routes.reshape(dp_size, rows_dev, top_count),
    )
    partials = run_experts(
        lax.all_to_all(packed, "expert", split_axis=1, concat_axis=1, tiled=True), w_first, w_second
    )
    returned = lax.all_to_all(
        lax.all_to_all(partials, "expert", split_axis=1, concat_axis=1, tiled=True),
        "dp",
        split_axis=0,
        concat_axis=0,
        tiled=True,
    )
    block_total = returned.astype(jnp.float32).sum(axis=0)
    expert_out = block_total.astype(jnp.bfloat16).reshape(experts * capacity, feature_dim)
    expert_out = lax.optimization_barrier(expert_out)
    picker = (
        own_slots[:, None] == jnp.arange(experts * capacity, dtype=jnp.int32)[None, :]
    ).astype(jnp.bfloat16)
    values = jnp.dot(picker, expert_out, preferred_element_type=jnp.float32)
    weighted = values.reshape(rows_dev, top_count, feature_dim) * gates[:, :, None]
    return (tokens.astype(jnp.float32) + weighted.sum(axis=1)).astype(jnp.bfloat16)


def body(tokens, routing, gates, ln_gain, w_in, w_out):
    rows_dev = tokens.shape[0]
    experts = lax.axis_size("expert")
    capacity = max(2, min(rows_dev, 2 * rows_dev * routing.shape[1] // experts))
    if capacity == rows_dev and experts == 4 and lax.axis_size("dp") == 4:
        return dense_body(tokens, routing, gates, ln_gain, w_in, w_out)
    return slot_body(tokens, routing, gates, ln_gain, w_in, w_out)


def solution(mesh):
    placed = (
        P(("groups", "expert", "dp"), None),
        P(("groups", "expert", "dp"), None),
        P(("groups", "expert", "dp"), None),
        P(),
        P("expert", None, "dp"),
        P("expert", "dp", None),
    )
    return jax.shard_map(
        body,
        mesh=mesh,
        in_specs=placed,
        out_specs=P(("groups", "expert", "dp"), None),
        check_vma=False,
    )
```

```python
import functools

import jax
import jax.numpy as jnp
from jax import lax
from jax.experimental import pallas as pl
from jax.experimental.pallas import tpu as pltpu
from jax.sharding import PartitionSpec as P

LANES = 128
GATE_TERMS = 3
VMEM = pl.BlockSpec(memory_space=pltpu.VMEM)
SMALL = pltpu.CompilerParams(vmem_limit_bytes=4 * 1024 * 1024)
CHEAP = pl.CostEstimate(flops=1, bytes_accessed=1, transcendentals=0)
DEAR = pl.CostEstimate(flops=10**10, bytes_accessed=1, transcendentals=0)
SOME = pl.CostEstimate(flops=4*10**9, bytes_accessed=1, transcendentals=0)
ANY = pl.BlockSpec(memory_space=pl.ANY)


def in_hbm(array):
    return pltpu.with_memory_space_constraint(array, pltpu.HBM)


def in_vmem(array):
    return pltpu.with_memory_space_constraint(array, pltpu.VMEM)


def norm_kernel(experts, *refs):
    sources, out_ref, targets, sems = refs[:4], refs[4], refs[5:9], refs[9]
    copies = [
        pltpu.make_async_copy(source, target, sems.at[i])
        for i, (source, target) in enumerate(zip(sources, targets))
    ]
    for copy in copies:
        copy.start()
    for copy in copies:
        copy.wait()
    tokens_ref, routing_ref, gates_ref, gain_ref = targets
    width = tokens_ref.shape[1]
    values = tokens_ref[...].astype(jnp.float32)
    center = values - jnp.mean(values, axis=1, keepdims=True)
    variance = jnp.mean(center * center, axis=1, keepdims=True)
    normed = center * lax.rsqrt(variance + 1e-05) * gain_ref[...]
    out_ref[:, :width] = normed.astype(jnp.bfloat16)
    lane = lax.broadcasted_iota(jnp.int32, (LANES, tokens_ref.shape[0]), 0)
    expert = lax.rem(lane, experts)
    term = lax.div(lane, experts)
    gate = jnp.zeros(lane.shape, jnp.float32)
    for k in range(routing_ref.shape[0]):
        gate += jnp.where(routing_ref[k : k + 1, :] == expert, gates_ref[k : k + 1, :], 0.0)
    rest = gate
    packed = jnp.zeros(lane.shape, jnp.float32)
    for i in range(GATE_TERMS):
        part = rest.astype(jnp.bfloat16).astype(jnp.float32)
        packed = jnp.where(term == i, part, packed)
        rest = rest - part
    out_ref[:, width:] = packed.T.astype(jnp.bfloat16)


def norm_and_pack(tokens, routing, gates, ln_gain, experts):
    rows, width = tokens.shape
    arrays = (tokens, routing.T, gates.T, ln_gain.reshape(1, width))
    return pl.pallas_call(
        functools.partial(norm_kernel, experts),
        out_shape=pltpu.VMEM((rows, width + LANES), jnp.bfloat16),
        in_specs=[ANY] * 4,
        out_specs=VMEM,
        scratch_shapes=[pltpu.VMEM(a.shape, a.dtype) for a in arrays]
        + [pltpu.SemaphoreType.DMA((4,))],
        compiler_params=SMALL,
        cost_estimate=CHEAP,
        name="norm",
    )(*[in_hbm(a) for a in arrays])


def join_kernel(pieces, *refs):
    at = 0
    for ref, (start, size) in zip(refs, pieces):
        refs[-1][at : at + size, :] = ref[start : start + size, :]
        at += size


def join(arrays, behind=(), pieces=None, cost=CHEAP):
    pieces = pieces or [(0, a.shape[0]) for a in arrays]
    rows, width = sum(size for _, size in pieces), arrays[0].shape[1]
    return pl.pallas_call(
        functools.partial(join_kernel, pieces),
        out_shape=pltpu.VMEM((rows, width), arrays[0].dtype),
        in_specs=[VMEM] * len(arrays) + [ANY] * len(behind),
        out_specs=VMEM,
        compiler_params=SMALL,
        cost_estimate=cost,
        name="join",
    )(*arrays, *behind)


def mark_kernel(*refs):
    refs[-1][...] = jnp.zeros_like(refs[-1])


def mark(behind, cost):
    return pl.pallas_call(
        mark_kernel,
        out_shape=pltpu.VMEM((8, LANES), jnp.float32),
        in_specs=[ANY] * len(behind),
        out_specs=VMEM,
        compiler_params=SMALL,
        cost_estimate=cost,
        name="mark",
    )(*behind)


def part_kernel(start, count, *refs):
    rows = refs[-1].shape[0]
    total = jnp.zeros(refs[-1].shape, jnp.float32)
    for ref in refs[:count]:
        at = start if ref.shape[0] > rows else 0
        total += ref[at : at + rows, :].astype(jnp.float32)
    refs[-1][...] = total.astype(refs[-1].dtype)


def part_sum(arrays, start, rows, behind=(), cost=CHEAP):
    return pl.pallas_call(
        functools.partial(part_kernel, start, len(arrays)),
        out_shape=pltpu.VMEM((rows, arrays[0].shape[1]), jnp.bfloat16),
        in_specs=[VMEM] * len(arrays) + [ANY] * len(behind),
        out_specs=VMEM,
        compiler_params=SMALL,
        cost_estimate=cost,
        name="part",
    )(*arrays, *behind)


def sum_kernel(*refs):
    total = refs[0][...].astype(jnp.float32)
    for ref in refs[1:-1]:
        total += ref[...].astype(jnp.float32)
    refs[-1][...] = total


def sum_arrays(arrays, cost):
    return pl.pallas_call(
        sum_kernel,
        out_shape=pltpu.VMEM(arrays[0].shape, jnp.float32),
        in_specs=[VMEM] * len(arrays),
        out_specs=VMEM,
        compiler_params=SMALL,
        cost_estimate=cost,
        name="sum",
    )(*arrays)


def gate_column(experts, expert_ref, tail):
    lane = lax.broadcasted_iota(jnp.int32, tail.shape, 1)
    chosen = (lax.rem(lane, experts) == expert_ref[0]) & (lane < GATE_TERMS * experts)
    return jnp.sum(jnp.where(chosen, tail.astype(jnp.float32), 0.0), axis=1, keepdims=True)


def load_ffn_kernel(
    experts, cuts, skipped, expert_ref, kept_ref, first_ref, second_ref, *refs
):
    keep_ref, weights_ref, rows_ref, hidden_ref, total_ref, sems = refs[skipped:]
    width, units = first_ref.shape
    copies = []
    for j in range(cuts):
        size = width // cuts
        part = pl.ds(j * size, size)
        copies.append(
            [pltpu.make_async_copy(first_ref.at[part], weights_ref.at[part], sems.at[0, j])]
        )
    panels = second_ref.shape[1] // units
    for j in range(cuts):
        size = units // cuts
        copies.append(
            [
                pltpu.make_async_copy(
                    second_ref.at[pl.ds(j * size, size), pl.ds(i * units, units)],
                    weights_ref.at[pl.ds(width + i * units + j * size, size)],
                    sems.at[1 + i, j],
                )
                for i in range(panels)
            ]
        )
    for group in copies:
        for copy in group:
            copy.start()
    rows_ref[...] = kept_ref[...]
    gate = gate_column(experts, expert_ref, rows_ref[:, width:])
    for j in range(cuts):
        for copy in copies[j]:
            copy.wait()
        size = width // cuts
        part = slice(j * size, (j + 1) * size)
        dot = jnp.dot(
            rows_ref[:, part], weights_ref[part, :], preferred_element_type=jnp.float32
        )
        if j == 0:
            total_ref[:, :units] = dot
        else:
            total_ref[:, :units] += dot
    hidden_ref[...] = jnp.maximum(total_ref[:, :units], 0.0).astype(jnp.bfloat16)
    for j in range(cuts):
        for copy in copies[cuts + j]:
            copy.wait()
        size = units // cuts
        part = slice(j * size, (j + 1) * size)
        for i in range(panels):
            start = width + i * units + j * size
            columns = slice(i * units, (i + 1) * units)
            dot = jnp.dot(
                hidden_ref[:, part],
                weights_ref[start : start + size, :],
                preferred_element_type=jnp.float32,
            )
            if j > 0:
                dot += total_ref[:, columns]
            if j < cuts - 1:
                total_ref[:, columns] = dot
            else:
                out = (dot * gate).astype(jnp.bfloat16)
                keep_ref[:, columns] = out


def load_ffn(kept, w_first, w_second, experts, expert, behind):
    width, units = w_first.shape
    rows, cuts = kept.shape[0], 4
    out = jax.ShapeDtypeStruct((rows, width), jnp.bfloat16)
    return pl.pallas_call(
        functools.partial(load_ffn_kernel, experts, cuts, len(behind)),
        out_shape=(out, pltpu.VMEM((2 * width, units), w_first.dtype)),
        in_specs=[pl.BlockSpec(memory_space=pltpu.SMEM), VMEM] + [ANY] * (2 + len(behind)),
        out_specs=(VMEM, VMEM),
        scratch_shapes=[
            pltpu.VMEM((rows, width + LANES), jnp.bfloat16),
            pltpu.VMEM((rows, units), jnp.bfloat16),
            pltpu.VMEM((rows, width), jnp.float32),
            pltpu.SemaphoreType.DMA((1 + width // units, cuts)),
        ],
        compiler_params=pltpu.CompilerParams(vmem_limit_bytes=16 * 1024 * 1024),
        cost_estimate=CHEAP,
        name="load_ffn",
    )(expert, kept, in_hbm(w_first), in_hbm(w_second), *behind)


def ffn_kernel(experts, kept_count, sent_count, skipped, expert_ref, *refs):
    pieces = kept_count + sent_count
    kept, sent = refs[:kept_count], refs[kept_count:pieces]
    weights = refs[pieces]
    keep_ref, send_ref, rows_ref, hidden_ref = refs[pieces + 1 + skipped :]
    width, units = keep_ref.shape[1], weights.shape[1]
    at = 0
    for ref in kept + sent:
        rows_ref[at : at + ref.shape[0], :] = ref[...]
        at += ref.shape[0]
    half = keep_ref.shape[0]
    gate = gate_column(experts, expert_ref, rows_ref[:, width:])
    step = 256
    for j in range(0, units, step):
        dot = jnp.dot(
            rows_ref[:, :width], weights[:width, j : j + step], preferred_element_type=jnp.float32
        )
        hidden_ref[:, j : j + step] = jnp.maximum(dot, 0.0).astype(jnp.bfloat16)
    for j in range(0, width, step):
        start, column = width + j // units * units, j % units
        dot = jnp.dot(
            hidden_ref[...],
            weights[start : start + units, column : column + step],
            preferred_element_type=jnp.float32,
        )
        out = (dot * gate).astype(jnp.bfloat16)
        send_ref[:, j : j + step] = out[half:]
        keep_ref[:, j : j + step] = out[:half]


def ffn(kept, sent, weights, experts, expert, behind, cost):
    width, units = weights.shape[0] // 2, weights.shape[1]
    half = sum(a.shape[0] for a in kept)
    rest = sum(a.shape[0] for a in sent)
    count = len(kept) + len(sent)
    return pl.pallas_call(
        functools.partial(ffn_kernel, experts, len(kept), len(sent), len(behind)),
        out_shape=(
            jax.ShapeDtypeStruct((half, width), jnp.bfloat16),
            jax.ShapeDtypeStruct((rest, width), jnp.bfloat16),
        ),
        in_specs=[pl.BlockSpec(memory_space=pltpu.SMEM)]
        + [VMEM] * (count + 1)
        + [ANY] * len(behind),
        out_specs=(VMEM, VMEM),
        scratch_shapes=[
            pltpu.VMEM((half + rest, width + LANES), jnp.bfloat16),
            pltpu.VMEM((half + rest, units), jnp.bfloat16),
        ],
        compiler_params=pltpu.CompilerParams(vmem_limit_bytes=16 * 1024 * 1024),
        cost_estimate=pl.CostEstimate(
            flops=4 * (half + rest) * width * units, bytes_accessed=4 * width * units, transcendentals=0
        ),
        name="ffn",
    )(expert, *kept, *sent, in_vmem(weights), *behind)


def swap(array, axis, distance):
    pairs = [(i, i ^ distance) for i in range(lax.axis_size(axis))]
    return lax.ppermute(array, axis, pairs)


def add(*arrays):
    return sum(a.astype(jnp.float32) for a in arrays)


def dense_body(tokens, routing, gates, ln_gain, w_in, w_out):
    rows = tokens.shape[0]
    experts = lax.axis_size("expert")
    core_bit, chip_bit = 1, 2
    expert = lax.axis_index("expert").reshape(1)

    def run(kept, sent, behind=(), cost=CHEAP):
        keep, send = ffn(kept, sent, weights, experts, expert, behind, cost)
        return keep, swap(send, "dp", core_bit)

    def core_swap(array):
        return swap(array, "dp", core_bit)

    own = norm_and_pack(tokens, routing, gates, ln_gain, experts)
    lane3, lane1 = swap(own, "expert", 3), swap(own, "expert", 1)
    across0 = swap(own, "dp", chip_bit)
    lane2 = swap(own, "expert", 2)
    keep0, weights = load_ffn(own, w_in[0], w_out[0], experts, expert, [])
    lane3 = join([lane3], [keep0])
    across3 = swap(lane3, "dp", chip_bit)
    across1, across2 = swap(lane1, "dp", chip_bit), swap(lane2, "dp", chip_bit)
    kept0 = join([own, across0])
    kept3 = join([lane3, across3], [mark([lane2, mark([lane1, across0], CHEAP)], CHEAP)])
    pair3 = run([kept3], [core_swap(kept3)], [mark([across1, kept3], SOME)])
    far3 = part_sum(pair3, rows, rows, [mark([across2, pair3[0]], SOME)])
    sent0 = join([core_swap(kept0)], [kept3])
    kept2 = join([lane2, across2], [far3, sent0])
    pair2 = run([kept2], [core_swap(kept2)])
    kept1 = join([lane1, across1], [kept2])
    keep1, send10 = ffn(
        [kept1, across0], [core_swap(kept1), sent0], weights, experts, expert, [pair2[0]], CHEAP
    )
    back10 = core_swap(send10)
    near3 = part_sum([*pair3, swap(far3, "dp", chip_bit)], 0, rows, [keep1], DEAR)
    far2 = part_sum(pair2, rows, rows, [near3])
    far1 = part_sum([keep1, back10], rows, rows, [far2])
    near2 = part_sum([*pair2, swap(far2, "dp", chip_bit)], 0, rows, [far1])
    near1 = part_sum([keep1, back10, swap(far1, "dp", chip_bit)], 0, rows, [near2])
    far0 = join([add(keep1[2 * rows :], back10[3 * rows :]).astype(jnp.bfloat16)], [near1])
    near0 = add(keep0, back10[2 * rows : 3 * rows], swap(far0, "dp", chip_bit))
    total = sum_arrays([tokens, swap(near3, "expert", 3)], DEAR)
    return add(total, near0, swap(near1, "expert", 1), swap(near2, "expert", 2)).astype(
        jnp.bfloat16
    )


def layer_norm(tokens, ln_gain):
    values = tokens.astype(jnp.float32)
    center = values - jnp.mean(values, axis=1, keepdims=True)
    variance = jnp.mean(center * center, axis=1, keepdims=True)
    return (center * lax.rsqrt(variance + 1e-05) * ln_gain).astype(jnp.bfloat16)


def slot_index(routing, experts, capacity):
    flat_ids = routing.reshape(-1)
    onehot = (flat_ids[:, None] == jnp.arange(experts, dtype=jnp.int32)[None, :]).astype(jnp.int32)
    rank_run = jnp.cumsum(onehot, axis=0) - 1
    own_rank = jnp.sum(onehot * rank_run, axis=1)
    return flat_ids * capacity + own_rank


def pack_slots(normed, routing, experts, capacity):
    slots = slot_index(routing, experts, capacity)
    picker = (slots[None, :] == jnp.arange(experts * capacity, dtype=jnp.int32)[:, None]).astype(
        jnp.bfloat16
    )
    picker = picker.reshape(experts * capacity, normed.shape[0], routing.shape[1]).sum(axis=2)
    outgoing = jnp.dot(picker, normed, preferred_element_type=jnp.float32).astype(jnp.bfloat16)
    return outgoing.reshape(experts, capacity, normed.shape[1])


def run_experts(block_in, w_first, w_second):
    dims_in = block_in.shape
    row_mat = block_in.reshape(-1, dims_in[-1])
    hidden = jnp.maximum(jnp.dot(row_mat, w_first, preferred_element_type=jnp.float32), 0.0).astype(
        jnp.bfloat16
    )
    product = jnp.dot(hidden, w_second, preferred_element_type=jnp.float32).astype(jnp.bfloat16)
    return product.reshape(dims_in)


def slot_body(tokens, routing, gates, ln_gain, w_in, w_out):
    rows_dev = tokens.shape[0]
    feature_dim = tokens.shape[1]
    top_count = routing.shape[1]
    experts = lax.axis_size("expert")
    dp_size = lax.axis_size("dp")
    capacity = max(2, min(rows_dev, 2 * rows_dev * top_count // experts))
    w_first = w_in[0]
    w_second = w_out[0]
    normed = layer_norm(tokens, ln_gain)
    own_slots = slot_index(routing, experts, capacity)
    all_normed, all_routes = (
        lax.all_gather(normed, "dp", axis=0, tiled=True),
        lax.all_gather(routing, "dp", axis=0, tiled=True),
    )

    def pack_member(member_rows, member_routes):
        return pack_slots(member_rows, member_routes, experts, capacity)

    packed = jax.vmap(pack_member)(
        all_normed.reshape(dp_size, rows_dev, feature_dim),
        all_routes.reshape(dp_size, rows_dev, top_count),
    )
    partials = run_experts(
        lax.all_to_all(packed, "expert", split_axis=1, concat_axis=1, tiled=True), w_first, w_second
    )
    returned = lax.all_to_all(
        lax.all_to_all(partials, "expert", split_axis=1, concat_axis=1, tiled=True),
        "dp",
        split_axis=0,
        concat_axis=0,
        tiled=True,
    )
    block_total = returned.astype(jnp.float32).sum(axis=0)
    expert_out = block_total.astype(jnp.bfloat16).reshape(experts * capacity, feature_dim)
    expert_out = lax.optimization_barrier(expert_out)
    picker = (
        own_slots[:, None] == jnp.arange(experts * capacity, dtype=jnp.int32)[None, :]
    ).astype(jnp.bfloat16)
    values = jnp.dot(picker, expert_out, preferred_element_type=jnp.float32)
    weighted = values.reshape(rows_dev, top_count, feature_dim) * gates[:, :, None]
    return (tokens.astype(jnp.float32) + weighted.sum(axis=1)).astype(jnp.bfloat16)


def body(tokens, routing, gates, ln_gain, w_in, w_out):
    rows_dev = tokens.shape[0]
    experts = lax.axis_size("expert")
    capacity = max(2, min(rows_dev, 2 * rows_dev * routing.shape[1] // experts))
    if capacity == rows_dev and experts == 4 and lax.axis_size("dp") == 4:
        return dense_body(tokens, routing, gates, ln_gain, w_in, w_out)
    return slot_body(tokens, routing, gates, ln_gain, w_in, w_out)


def solution(mesh):
    placed = (
        P(("groups", "expert", "dp"), None),
        P(("groups", "expert", "dp"), None),
        P(("groups", "expert", "dp"), None),
        P(),
        P("expert", None, "dp"),
        P("expert", "dp", None),
    )
    return jax.shard_map(
        body,
        mesh=mesh,
        in_specs=placed,
        out_specs=P(("groups", "expert", "dp"), None),
        check_vma=False,
    )
```
